32 devices in a mesh: grp: 2 (over core), blk: 16 (over z, y, x).
Axes of the slice: x: 2, y: 2, z: 4, core: 2. Of those that a mesh axis runs over, the one named last changes fastest.
Arguments:
- queries: bfloat16 [256, 4096], P('blk'), may hold values from -30 to 30
- turn_pos: int32 [256], P('blk'), may hold values from 32768 to 33280, as said below
- cached_key_rows: bfloat16 [65536, 1024], P(('grp', 'blk')), may hold values from -21 to 21
- cached_value_rows: bfloat16 [65536, 1024], P(('grp', 'blk')), may hold values from -6 to 6
- turn_keys: bfloat16 [256, 1024], P(('grp', 'blk')), may hold values from -33 to 33
- turn_values: bfloat16 [256, 1024], P(('grp', 'blk')), may hold values from -6 to 6
- cache_pos: int32 [65536], P(('grp', 'blk')), may hold values from 0 to 65535, each once
Outputs:
- attended: bfloat16 [256, 4096], P('blk')
The draws below stay inside these ranges and needn't reach their ends.
Inputs may be any that keep to these rules, and one draw needn't show every extreme that they name: turn_pos rises strictly by one or two from each token to the next.
All inputs are finite; a program needn't handle non-finite values.
Results may differ from the reference program's by a relative error of at most 0.0026.
Values may be sent and summed in bfloat16 or wider, within the bound.
A program may use at most 128 MiB of HBM per device.

```python
import math
import jax
import jax.numpy as jnp
from jax import lax

QUERY_HEADS = 32
KEY_VALUE_HEADS = 8
HEAD_SIZE = 128
TURN_TOKENS = 256
CACHE_SLOTS = 65536


def shared_turn(key):
    query_group = QUERY_HEADS // KEY_VALUE_HEADS
    key_query_scores = jax.random.fold_in(key, 11)
    key_counter = jax.random.fold_in(key, 12)
    turn_key_rows = 3.5 * jax.random.truncated_normal(key_counter, -6.0, 6.0, (TURN_TOKENS, KEY_VALUE_HEADS, HEAD_SIZE), jnp.float32)
    query_everything = jax.random.truncated_normal(key_query_scores, -6.0, 6.0, (TURN_TOKENS, KEY_VALUE_HEADS, query_group, HEAD_SIZE), jnp.float32)
    return (query_everything, turn_key_rows)


def draw_queries(key, part):
    query_everything, turn_key_rows = shared_turn(key)
    return query_everything.reshape(TURN_TOKENS, QUERY_HEADS * HEAD_SIZE).astype(jnp.bfloat16)


def draw_turn_keys(key, part):
    query_everything, turn_key_rows = shared_turn(key)
    return turn_key_rows.reshape(TURN_TOKENS, KEY_VALUE_HEADS * HEAD_SIZE).astype(jnp.bfloat16)


def draw_turn_pos(key, part):
    kstep = jax.random.fold_in(key, 22)
    gaps = jax.random.randint(kstep, (TURN_TOKENS,), 1, 3)
    gaps = gaps.at[0].set(0)
    rising = jnp.cumsum(gaps)
    finish = CACHE_SLOTS // 2 + 2 * TURN_TOKENS
    return (finish - rising[TURN_TOKENS - 1] + rising).astype(jnp.int32)


def shard_levels(own_key, dims, split, low, largest):
    loudness, own = 1.0, jax.random.fold_in(own_key, 6)
    for position, parts in split:
        heights = jnp.exp(jax.random.uniform(jax.random.fold_in(own, position), (parts,), jnp.float32, low / len(split), largest / len(split)))
        loudness = loudness * jnp.repeat(heights, dims[position] // parts).reshape([-1 if axis == position else 1 for axis in range(len(dims))])
    return loudness


def noise(own_key, shape, width, most, split=(), kind=jnp.bfloat16):
    values = jax.random.normal(own_key, shape, jnp.float32) * width
    if len(split) > 0:
        values = shard_levels(own_key, shape, split, -0.22, 0.18) * values
    return jnp.clip(values, min=-most, max=most).astype(kind)


def setup_inputs(seed: int = 0) -> dict:
    streams_of = jax.random.split(jax.random.key(seed), 8)
    return {
        "queries": draw_queries(jax.random.fold_in(streams_of[7], 71), 0),
        "turn_pos": draw_turn_pos(jax.random.fold_in(streams_of[7], 71), 0),
        "cached_key_rows": noise(streams_of[2], (CACHE_SLOTS, KEY_VALUE_HEADS * HEAD_SIZE), 3.5, 21.0, ((0, 32),)),
        "cached_value_rows": noise(streams_of[3], (CACHE_SLOTS, KEY_VALUE_HEADS * HEAD_SIZE), 1.0, 6.0, ((0, 32),)),
        "turn_keys": draw_turn_keys(jax.random.fold_in(streams_of[7], 71), 0),
        "turn_values": noise(streams_of[5], (TURN_TOKENS, KEY_VALUE_HEADS * HEAD_SIZE), 1.0, 6.0, ((0, 32),)),
        "cache_pos": jax.random.permutation(streams_of[6], CACHE_SLOTS).astype(jnp.int32),
    }


NEGATIVE_FLOOR = -1e+30

def reference(queries, turn_pos, cached_key_rows, cached_value_rows, turn_keys, turn_values, cache_pos):
    query_group = QUERY_HEADS // KEY_VALUE_HEADS
    scale = 1.0 / math.sqrt(HEAD_SIZE)
    query_block = 16
    cached_key_view = cached_key_rows.astype(jnp.float32).reshape(CACHE_SLOTS, KEY_VALUE_HEADS, HEAD_SIZE)
    cached_value_view = cached_value_rows.astype(jnp.float32).reshape(CACHE_SLOTS, KEY_VALUE_HEADS, HEAD_SIZE)
    turn_key_view = turn_keys.astype(jnp.float32).reshape(TURN_TOKENS, KEY_VALUE_HEADS, HEAD_SIZE)
    turn_value_view = turn_values.astype(jnp.float32).reshape(TURN_TOKENS, KEY_VALUE_HEADS, HEAD_SIZE)
    query_stack = queries.astype(jnp.float32).reshape(TURN_TOKENS // query_block, query_block, KEY_VALUE_HEADS, query_group, HEAD_SIZE)
    posall = turn_pos.reshape(TURN_TOKENS // query_block, query_block)
    rowall = jnp.arange(TURN_TOKENS, dtype=jnp.int32).reshape(TURN_TOKENS // query_block, query_block)
    newidx = jnp.arange(TURN_TOKENS, dtype=jnp.int32)

    def one(items):
        qb, pb, rb = items
        sc = jnp.einsum('tkgd,ckd->tkgc', qb, cached_key_view) * scale
        sn = jnp.einsum('tkgd,jkd->tkgj', qb, turn_key_view) * scale
        mc = (cache_pos[None, :] < pb[:, None])[:, None, None, :]
        mn = (newidx[None, :] <= rb[:, None])[:, None, None, :]
        top = jnp.maximum(lax.optimization_barrier(jnp.max(jnp.where(mc, sc, NEGATIVE_FLOOR), -1)), lax.optimization_barrier(jnp.max(jnp.where(mn, sn, NEGATIVE_FLOOR), -1)))
        pc = jnp.where(mc, jnp.exp(sc - top[..., None]), 0.0)
        pn = jnp.where(mn, jnp.exp(sn - top[..., None]), 0.0)
        den = lax.optimization_barrier(jnp.sum(pc, -1)) + lax.optimization_barrier(jnp.sum(pn, -1))
        pcb = lax.optimization_barrier(pc.astype(jnp.bfloat16)).astype(jnp.float32)
        pnb = lax.optimization_barrier(pn.astype(jnp.bfloat16)).astype(jnp.float32)
        num = jnp.einsum('tkgc,ckd->tkgd', pcb, cached_value_view) + jnp.einsum('tkgj,jkd->tkgd', pnb, turn_value_view)
        return (num / den[..., None]).astype(jnp.bfloat16).reshape(query_block, QUERY_HEADS * HEAD_SIZE)
    return lax.map(one, (query_stack, posall, rowall)).reshape(TURN_TOKENS, QUERY_HEADS * HEAD_SIZE)
```

```python
import functools
import math

import jax
import jax.numpy as jnp
from jax import lax
from jax.experimental import pallas as pl
from jax.experimental.pallas import tpu as pltpu
from jax.sharding import PartitionSpec as P

QUERY_HEADS = 32
KEY_VALUE_HEADS = 8
HEAD_SIZE = 128
GROUP = QUERY_HEADS // KEY_VALUE_HEADS
LANE = 128
BLOCK = 256
TURN_SPAN = 512
FAR = 1e9
LOW = -1e30
LOG2E = math.log2(math.e)
NT = (((1,), (1,)), ((), ()))


def _dot(a, b):
    return jnp.dot(a, b, preferred_element_type=jnp.float32)


def _dot_nt(a, b):
    return lax.dot_general(a, b, NT, preferred_element_type=jnp.float32)


def _rank(flags, slots):
    rows = slots // LANE
    upper = (
        lax.broadcasted_iota(jnp.int32, (LANE, LANE), 0)
        < lax.broadcasted_iota(jnp.int32, (LANE, LANE), 1)
    ).astype(jnp.bfloat16)
    inside = _dot(flags.astype(jnp.bfloat16), upper)
    counts = jnp.sum(flags, axis=1, keepdims=True)
    before = (
        lax.broadcasted_iota(jnp.int32, (rows, rows), 1)
        < lax.broadcasted_iota(jnp.int32, (rows, rows), 0)
    ).astype(jnp.bfloat16)
    ahead = _dot(before, jnp.broadcast_to(counts, (rows, LANE)).astype(jnp.bfloat16))
    return inside + ahead, jnp.sum(flags)


def _compact_kernel(
    base, slots, fresh, pos_ref, k_ref, v_ref, tk_ref, tv_ref, kc_ref, vc_ref, code_ref, count_ref
):
    pos = pos_ref[...] - base
    always = (pos < 0).astype(jnp.float32)
    maybe = ((pos >= 0) & (pos < TURN_SPAN)).astype(jnp.float32)
    rank_a, count_a = _rank(always, slots)
    rank_m, count_m = _rank(maybe, slots)
    count_a = count_a.astype(jnp.int32)
    count_m = count_m.astype(jnp.int32)
    count_ref[0] = count_a
    count_ref[1] = count_m
    dest_a = jnp.where(always > 0, rank_a.astype(jnp.int32), -1)
    dest_m = jnp.where(maybe > 0, rank_m.astype(jnp.int32) + count_a, -1)
    row_total = jnp.sum(always, axis=1, keepdims=True)
    del row_total
    kc_ref[pl.ds(0, LANE), :] = jnp.zeros((LANE, kc_ref.shape[1]), kc_ref.dtype)
    vc_ref[pl.ds(0, LANE), :] = jnp.zeros((LANE, vc_ref.shape[1]), vc_ref.dtype)
    window = BLOCK + LANE
    lanes = BLOCK // LANE
    for b in range(slots // BLOCK):
        start = jnp.sum(always[: b * lanes]).astype(jnp.int32) if b else jnp.int32(0)
        off = pl.multiple_of((start // LANE) * LANE, LANE)
        rows = lax.broadcasted_iota(jnp.int32, (window, LANE), 0) + off
        pick = jnp.concatenate(
            [
                (dest_a[b * lanes + i : b * lanes + i + 1, :] == rows)
                for i in range(lanes)
            ],
            axis=1,
        ).astype(jnp.float32).astype(jnp.bfloat16)
        for src, dst in ((k_ref, kc_ref), (v_ref, vc_ref)):
            got = _dot(pick, src[pl.ds(b * BLOCK, BLOCK), :]).astype(jnp.bfloat16)
            dst[pl.ds(off, LANE), :] = dst[pl.ds(off, LANE), :] + got[:LANE]
            dst[pl.ds(off + LANE, BLOCK), :] = got[LANE:]
    first = (count_a // LANE) * LANE
    for dst in (kc_ref, vc_ref):
        tail = pl.multiple_of(first + LANE, LANE)
        dst[pl.ds(tail, BLOCK), :] = jnp.zeros((BLOCK, dst.shape[1]), dst.dtype)
    total = count_a + count_m + fresh
    code = jnp.where(maybe > 0, pos + 1, 0)
    high, low = code // 32, code % 32

    def step(i, carry):
        off = pl.multiple_of(first + i * LANE, LANE)
        rows = lax.broadcasted_iota(jnp.int32, (LANE, LANE), 0) + off
        pick = jnp.concatenate(
            [(dest_m[j : j + 1, :] == rows) for j in range(slots // LANE)], axis=1
        ).astype(jnp.float32).astype(jnp.bfloat16)
        which = lax.broadcasted_iota(jnp.int32, (LANE, LANE), 1)
        turn_pick = (
            (which + (count_a + count_m) == rows) & (which < fresh)
        ).astype(jnp.float32).astype(jnp.bfloat16)
        keep = jnp.where(i == 0, 1.0, 0.0).astype(jnp.bfloat16)
        for src, turn, dst in ((k_ref, tk_ref, kc_ref), (v_ref, tv_ref, vc_ref)):
            got = (_dot(pick, src[...]) + _dot(turn_pick, turn[...])).astype(jnp.bfloat16)
            dst[pl.ds(off, LANE), :] = dst[pl.ds(off, LANE), :] * keep + got
            dst[pl.ds(off + LANE, BLOCK), :] = jnp.zeros((BLOCK, dst.shape[1]), dst.dtype)
        flat = jnp.concatenate([high[j : j + 1, :] for j in range(slots // LANE)], axis=1)
        flat_low = jnp.concatenate([low[j : j + 1, :] for j in range(slots // LANE)], axis=1)
        width = flat.shape[1]
        digits = jnp.concatenate(
            [jnp.broadcast_to(flat * 1.0, (8, width)), jnp.broadcast_to(flat_low * 1.0, (8, width))],
            axis=0,
        ).astype(jnp.bfloat16)
        got = _dot_nt(digits, pick)
        value = got[:8] * 32.0 + got[8:]
        place = lax.broadcasted_iota(jnp.int32, (8, LANE), 1) + off
        value = jnp.where(place < count_a, 0.0, jnp.where(place < count_a + count_m, value, FAR))
        code_ref[0:8, pl.ds(off, LANE)] = value
        turn_value = jnp.where(
            (place >= count_a + count_m) & (place < total),
            (place - (count_a + count_m)).astype(jnp.float32),
            FAR,
        )
        code_ref[8:16, pl.ds(off, LANE)] = turn_value
        return carry

    code_ref[...] = jnp.full(code_ref.shape, FAR, jnp.float32)
    lax.fori_loop(0, (total - first + LANE - 1) // LANE, step, 0)


def _attend_kernel(
    fresh, count_ref, q_ref, kc_ref, vc_ref, code_ref, lim_ref, out_ref, lse_ref, s_ref, m_ref, l_ref
):
    tokens = q_ref.shape[0]
    rows = GROUP * tokens
    heads = KEY_VALUE_HEADS
    factor = LOG2E / math.sqrt(HEAD_SIZE)
    count_a = count_ref[0]
    total = count_a + count_ref[1] + fresh
    plain = count_a // LANE
    chunks = (total + LANE - 1) // LANE

    lse_ref[...] = jnp.zeros_like(lse_ref)

    for k in range(heads):
        cols = slice(k * HEAD_SIZE, (k + 1) * HEAD_SIZE)
        m_ref[...] = jnp.full(m_ref.shape, LOW, jnp.float32)
        l_ref[...] = jnp.zeros_like(l_ref)

        def scores(i, masked):
            off = pl.multiple_of(i * LANE, LANE)
            key = kc_ref[pl.ds(off, LANE), cols]
            if masked:
                a = code_ref[0:1, pl.ds(off, LANE)]
                b = code_ref[8:9, pl.ds(off, LANE)]
                seen = (a < lim_ref[:, 0:1]) | (b < lim_ref[:, 1:2])
            for g in range(GROUP):
                h = k * GROUP + g
                s = _dot_nt(q_ref[:, h * HEAD_SIZE : (h + 1) * HEAD_SIZE], key)
                if masked:
                    s = jnp.where(seen, s, LOW)
                here = slice(g * tokens, (g + 1) * tokens)
                s_ref[i, here, :] = s
                m_ref[here, :] = jnp.maximum(m_ref[here, :], s)

        def open_body(i, c):
            scores(i, False)
            return c

        def masked_body(i, c):
            scores(i, True)
            return c

        lax.fori_loop(0, plain, open_body, 0)
        lax.fori_loop(plain, chunks, masked_body, 0)
        top = jnp.max(m_ref[...], axis=1, keepdims=True)
        m_ref[...] = jnp.broadcast_to(jnp.maximum(top, 0.1 * LOW), m_ref.shape)
        for g in range(GROUP):
            h = k * GROUP + g
            out_ref[:, h * HEAD_SIZE : (h + 1) * HEAD_SIZE] = jnp.zeros((tokens, HEAD_SIZE), jnp.float32)

        def weigh(i, c):
            off = pl.multiple_of(i * LANE, LANE)
            value = vc_ref[pl.ds(off, LANE), cols]
            for g in range(GROUP):
                h = k * GROUP + g
                here = slice(g * tokens, (g + 1) * tokens)
                w = jnp.exp2((s_ref[i, here, :] - m_ref[here, :]) * factor)
                l_ref[here, :] += w
                out_ref[:, h * HEAD_SIZE : (h + 1) * HEAD_SIZE] += _dot(w.astype(jnp.bfloat16), value)
            return c

        lax.fori_loop(0, chunks, weigh, 0)
        for g in range(GROUP):
            h = k * GROUP + g
            here = slice(g * tokens, (g + 1) * tokens)
            den = jnp.sum(l_ref[here, :], axis=1, keepdims=True)
            lane = lax.broadcasted_iota(jnp.int32, (tokens, LANE), 1)
            lse_ref[:, 0:LANE] = jnp.where(lane == h, m_ref[here, :] * factor, lse_ref[:, 0:LANE])
            lse_ref[:, LANE:] = jnp.where(lane == h, den, lse_ref[:, LANE:])


def on_device(
    queries, turn_pos, cached_key_rows, cached_value_rows, turn_keys, turn_values, cache_pos
):
    blk = lax.axis_size("blk")
    grp = lax.axis_size("grp")
    slots = cached_key_rows.shape[0]
    width = cached_key_rows.shape[1]
    fresh = turn_keys.shape[0]
    base = slots * grp * blk // 2
    size = -(-(slots + fresh) // LANE) * LANE + 2 * BLOCK
    every_query = lax.all_gather(queries, "blk", axis=0, tiled=True)
    all_pos = lax.all_gather(turn_pos, "blk", axis=0, tiled=True)
    tokens = every_query.shape[0]
    pad = ((0, LANE - fresh), (0, 0))
    vmem = pl.BlockSpec(memory_space=pltpu.VMEM)
    smem = pl.BlockSpec(memory_space=pltpu.SMEM)
    kc, vc, code, count = pl.pallas_call(
        functools.partial(_compact_kernel, base, slots, fresh),
        out_shape=(
            jax.ShapeDtypeStruct((size, width), jnp.bfloat16),
            jax.ShapeDtypeStruct((size, width), jnp.bfloat16),
            jax.ShapeDtypeStruct((16, size), jnp.float32),
            jax.ShapeDtypeStruct((2,), jnp.int32),
        ),
        in_specs=[vmem] * 5,
        out_specs=(vmem, vmem, vmem, smem),
        compiler_params=pltpu.CompilerParams(vmem_limit_bytes=40 * 2**20),
        name="compact",
    )(
        cache_pos.reshape(slots // LANE, LANE),
        cached_key_rows,
        cached_value_rows,
        jnp.pad(turn_keys, pad),
        jnp.pad(turn_values, pad),
    )
    rank = lax.axis_index(("grp", "blk"))
    limit = (all_pos - base + 1).astype(jnp.float32)
    index_limit = (jnp.arange(tokens, dtype=jnp.int32) - rank * fresh + 1).astype(jnp.float32)
    limits = jnp.stack([limit, index_limit], axis=1)
    rows = GROUP * tokens
    accum, stats = pl.pallas_call(
        functools.partial(_attend_kernel, fresh),
        out_shape=(
            jax.ShapeDtypeStruct((tokens, QUERY_HEADS * HEAD_SIZE), jnp.float32),
            jax.ShapeDtypeStruct((tokens, 2 * LANE), jnp.float32),
        ),
        in_specs=[smem] + [vmem] * 5,
        out_specs=(vmem, vmem),
        scratch_shapes=[
            pltpu.VMEM((size // LANE, rows, LANE), jnp.float32),
            pltpu.VMEM((rows, LANE), jnp.float32),
            pltpu.VMEM((rows, LANE), jnp.float32),
        ],
        compiler_params=pltpu.CompilerParams(vmem_limit_bytes=56 * 2**20),
        name="attend",
    )(count, every_query, kc, vc, code, limits)
    top, den = stats[:, :QUERY_HEADS], stats[:, LANE : LANE + QUERY_HEADS]
    highest = lax.pmax(top, ("grp", "blk"))
    alpha = jnp.exp2(top - highest)
    scaled = accum.reshape(tokens, QUERY_HEADS, HEAD_SIZE) * alpha[..., None]
    flat = scaled.reshape(tokens, QUERY_HEADS * HEAD_SIZE)
    both = jnp.concatenate([flat, den * alpha, jnp.zeros((tokens, LANE - QUERY_HEADS))], axis=1)
    mine = lax.psum_scatter(both, "blk", scatter_dimension=0, tiled=True)
    mine = lax.psum(mine, "grp")
    rows_out = mine.shape[0]
    num = mine[:, : QUERY_HEADS * HEAD_SIZE].reshape(rows_out, QUERY_HEADS, HEAD_SIZE)
    dens = mine[:, QUERY_HEADS * HEAD_SIZE : QUERY_HEADS * HEAD_SIZE + QUERY_HEADS]
    result = num / dens[..., None]
    return result.reshape(rows_out, QUERY_HEADS * HEAD_SIZE).astype(jnp.bfloat16)


def solution(mesh):
    placed = (
        P("blk", None),
        P("blk"),
        P(("grp", "blk"), None),
        P(("grp", "blk"), None),
        P(("grp", "blk"), None),
        P(("grp", "blk"), None),
        P(("grp", "blk")),
    )
    return jax.shard_map(
        on_device, mesh=mesh, in_specs=placed, out_specs=P("blk", None), check_vma=False
    )
```

```python
import functools
import math

import jax
import jax.numpy as jnp
from jax import lax
from jax.experimental import pallas as pl
from jax.experimental.pallas import tpu as pltpu
from jax.sharding import PartitionSpec as P

QUERY_HEADS = 32
KEY_VALUE_HEADS = 8
HEAD_SIZE = 128
GROUP = QUERY_HEADS // KEY_VALUE_HEADS
LANE = 128
BLOCK = 256
TURN_SPAN = 512
FAR = 1e9
LOW = -1e30
TINY = 1e-30
MESH = pl.DeviceIdType.MESH
LOG2E = math.log2(math.e)
NT = (((1,), (1,)), ((), ()))


def _dot(a, b):
    return jnp.dot(a, b, preferred_element_type=jnp.float32)


def _dot_nt(a, b):
    return lax.dot_general(a, b, NT, preferred_element_type=jnp.float32)


def _rank(flags, slots):
    rows = slots // LANE
    upper = (
        lax.broadcasted_iota(jnp.int32, (LANE, LANE), 0)
        < lax.broadcasted_iota(jnp.int32, (LANE, LANE), 1)
    ).astype(jnp.bfloat16)
    inside = _dot(flags.astype(jnp.bfloat16), upper)
    counts = jnp.sum(flags, axis=1, keepdims=True)
    before = (
        lax.broadcasted_iota(jnp.int32, (rows, rows), 1)
        < lax.broadcasted_iota(jnp.int32, (rows, rows), 0)
    ).astype(jnp.bfloat16)
    ahead = _dot(before, jnp.broadcast_to(counts, (rows, LANE)).astype(jnp.bfloat16))
    return inside + ahead, jnp.sum(flags)


def _compact_kernel(
    base, slots, fresh, pos_ref, k_ref, v_ref, tk_ref, tv_ref, kc_ref, vc_ref, code_ref, count_ref
):
    pos = pos_ref[...] - base
    always = (pos < 0).astype(jnp.float32)
    maybe = ((pos >= 0) & (pos < TURN_SPAN)).astype(jnp.float32)
    rank_a, count_a = _rank(always, slots)
    rank_m, count_m = _rank(maybe, slots)
    count_a = count_a.astype(jnp.int32)
    count_m = count_m.astype(jnp.int32)
    count_ref[0] = count_a
    count_ref[1] = count_m
    dest_a = jnp.where(always > 0, rank_a.astype(jnp.int32), -1)
    dest_m = jnp.where(maybe > 0, rank_m.astype(jnp.int32) + count_a, -1)
    kc_ref[pl.ds(0, LANE), :] = jnp.zeros((LANE, kc_ref.shape[1]), kc_ref.dtype)
    vc_ref[pl.ds(0, LANE), :] = jnp.zeros((LANE, vc_ref.shape[1]), vc_ref.dtype)
    window = BLOCK + LANE
    lanes = BLOCK // LANE
    for b in range(slots // BLOCK):
        start = jnp.sum(always[: b * lanes]).astype(jnp.int32) if b else jnp.int32(0)
        off = pl.multiple_of((start // LANE) * LANE, LANE)
        rows = lax.broadcasted_iota(jnp.int32, (window, LANE), 0) + off
        pick = jnp.concatenate(
            [
                (dest_a[b * lanes + i : b * lanes + i + 1, :] == rows)
                for i in range(lanes)
            ],
            axis=1,
        ).astype(jnp.float32).astype(jnp.bfloat16)
        for src, dst in ((k_ref, kc_ref), (v_ref, vc_ref)):
            got = _dot(pick, src[pl.ds(b * BLOCK, BLOCK), :]).astype(jnp.bfloat16)
            dst[pl.ds(off, LANE), :] = dst[pl.ds(off, LANE), :] + got[:LANE]
            dst[pl.ds(off + LANE, BLOCK), :] = got[LANE:]
    first = (count_a // LANE) * LANE
    for dst in (kc_ref, vc_ref):
        tail = pl.multiple_of(first + LANE, LANE)
        dst[pl.ds(tail, BLOCK), :] = jnp.zeros((BLOCK, dst.shape[1]), dst.dtype)
    total = count_a + count_m + fresh
    code = jnp.where(maybe > 0, pos + 1, 0)
    high, low = code // 32, code % 32

    def step(i, carry):
        off = pl.multiple_of(first + i * LANE, LANE)
        rows = lax.broadcasted_iota(jnp.int32, (LANE, LANE), 0) + off
        pick = jnp.concatenate(
            [(dest_m[j : j + 1, :] == rows) for j in range(slots // LANE)], axis=1
        ).astype(jnp.float32).astype(jnp.bfloat16)
        which = lax.broadcasted_iota(jnp.int32, (LANE, LANE), 1)
        turn_pick = (
            (which + (count_a + count_m) == rows) & (which < fresh)
        ).astype(jnp.float32).astype(jnp.bfloat16)
        keep = jnp.where(i == 0, 1.0, 0.0).astype(jnp.bfloat16)
        for src, turn, dst in ((k_ref, tk_ref, kc_ref), (v_ref, tv_ref, vc_ref)):
            got = (_dot(pick, src[...]) + _dot(turn_pick, turn[...])).astype(jnp.bfloat16)
            dst[pl.ds(off, LANE), :] = dst[pl.ds(off, LANE), :] * keep + got
            dst[pl.ds(off + LANE, BLOCK), :] = jnp.zeros((BLOCK, dst.shape[1]), dst.dtype)
        flat = jnp.concatenate([high[j : j + 1, :] for j in range(slots // LANE)], axis=1)
        flat_low = jnp.concatenate([low[j : j + 1, :] for j in range(slots // LANE)], axis=1)
        width = flat.shape[1]
        digits = jnp.concatenate(
            [jnp.broadcast_to(flat * 1.0, (8, width)), jnp.broadcast_to(flat_low * 1.0, (8, width))],
            axis=0,
        ).astype(jnp.bfloat16)
        got = _dot_nt(digits, pick)
        value = got[:8] * 32.0 + got[8:]
        place = lax.broadcasted_iota(jnp.int32, (8, LANE), 1) + off
        value = jnp.where(place < count_a, 0.0, jnp.where(place < count_a + count_m, value, FAR))
        code_ref[0:8, pl.ds(off, LANE)] = value
        turn_value = jnp.where(
            (place >= count_a + count_m) & (place < total),
            (place - (count_a + count_m)).astype(jnp.float32),
            FAR,
        )
        code_ref[8:16, pl.ds(off, LANE)] = turn_value
        return carry

    code_ref[...] = jnp.full(code_ref.shape, FAR, jnp.float32)
    lax.fori_loop(0, (total - first + LANE - 1) // LANE, step, 0)


def _attend_kernel(
    fresh, count_ref, first_ref, q_ref, kc_ref, vc_ref, code_ref, lim_ref, out_ref, lse_ref, s_ref, m_ref, l_ref
):
    tokens = q_ref.shape[0]
    rows = GROUP * tokens
    heads = KEY_VALUE_HEADS
    factor = LOG2E / math.sqrt(HEAD_SIZE)
    count_a = count_ref[0]
    total = count_a + count_ref[1] + fresh
    plain = count_a // LANE
    chunks = (total + LANE - 1) // LANE

    lse_ref[...] = jnp.zeros_like(lse_ref)
    token = lax.broadcasted_iota(jnp.int32, (tokens, LANE), 0)
    turn_limit = (token - first_ref[0] + 1).astype(jnp.float32)

    for k in range(heads):
        cols = slice(k * HEAD_SIZE, (k + 1) * HEAD_SIZE)
        m_ref[...] = jnp.full(m_ref.shape, LOW, jnp.float32)
        l_ref[...] = jnp.zeros_like(l_ref)

        def scores(i, masked):
            off = pl.multiple_of(i * LANE, LANE)
            key = kc_ref[pl.ds(off, LANE), cols]
            if masked:
                a = code_ref[0:1, pl.ds(off, LANE)]
                b = code_ref[8:9, pl.ds(off, LANE)]
                seen = (a < lim_ref[...]) | (b < turn_limit)
            for g in range(GROUP):
                h = k * GROUP + g
                s = _dot_nt(q_ref[:, h * HEAD_SIZE : (h + 1) * HEAD_SIZE], key)
                if masked:
                    s = jnp.where(seen, s, LOW)
                here = slice(g * tokens, (g + 1) * tokens)
                s_ref[i, here, :] = s
                m_ref[here, :] = jnp.maximum(m_ref[here, :], s)

        def open_body(i, c):
            scores(i, False)
            return c

        def masked_body(i, c):
            scores(i, True)
            return c

        lax.fori_loop(0, plain, open_body, 0)
        lax.fori_loop(plain, chunks, masked_body, 0)
        top = jnp.max(m_ref[...], axis=1, keepdims=True)
        m_ref[...] = jnp.broadcast_to(jnp.maximum(top, 0.1 * LOW), m_ref.shape)
        for g in range(GROUP):
            h = k * GROUP + g
            out_ref[:, h * HEAD_SIZE : (h + 1) * HEAD_SIZE] = jnp.zeros((tokens, HEAD_SIZE), jnp.float32)

        def weigh(i, c):
            off = pl.multiple_of(i * LANE, LANE)
            value = vc_ref[pl.ds(off, LANE), cols]
            for g in range(GROUP):
                h = k * GROUP + g
                here = slice(g * tokens, (g + 1) * tokens)
                w = jnp.exp2((s_ref[i, here, :] - m_ref[here, :]) * factor)
                l_ref[here, :] += w
                out_ref[:, h * HEAD_SIZE : (h + 1) * HEAD_SIZE] += _dot(w.astype(jnp.bfloat16), value)
            return c

        lax.fori_loop(0, chunks, weigh, 0)
        for g in range(GROUP):
            h = k * GROUP + g
            here = slice(g * tokens, (g + 1) * tokens)
            den = jnp.sum(l_ref[here, :], axis=1, keepdims=True)
            lane = lax.broadcasted_iota(jnp.int32, (tokens, LANE), 1)
            both = jnp.where(lane == QUERY_HEADS + h, den, lse_ref[...])
            lse_ref[...] = jnp.where(lane == h, m_ref[here, :] * factor, both)
            hcols = slice(h * HEAD_SIZE, (h + 1) * HEAD_SIZE)
            out_ref[:, hcols] = out_ref[:, hcols] * (1.0 / jnp.maximum(den, TINY))


def _orders(grp_index, bits):
    odd = grp_index % 2
    if bits < 2:
        return [jnp.int32(2**b) for b in range(bits)]
    return [1 + odd, 2 - odd] + [jnp.int32(2**b) for b in range(2, bits)]


def _greet(me, grp_index, grp, worths):
    barrier = pltpu.get_barrier_semaphore()
    for w in worths:
        side = (me // w) % 2
        pl.semaphore_signal(
            barrier, inc=1, device_id=(grp_index, me + (1 - 2 * side) * w), device_id_type=MESH
        )
    for d in range(1, grp):
        pl.semaphore_signal(
            barrier, inc=1, device_id=((grp_index + d) % grp, me), device_id_type=MESH
        )
    pl.semaphore_wait(barrier, len(worths) + grp - 1)


def _gather_kernel(
    blk, grp, q_ref, p_ref, out_ref, pos_ref, local_sem, send_sem, recv_sem, psend, precv, csend, crecv
):
    me, mine = lax.axis_index("blk"), lax.axis_index("grp")
    bits = blk.bit_length() - 1
    worths = _orders(mine, bits)[::-1]
    width = q_ref.shape[1] // grp
    own = pltpu.make_async_copy(q_ref, out_ref.at[me], local_sem)
    own.start()
    pos_ref[me] = p_ref[...]
    _greet(me, mine, grp, worths)
    own.wait()
    cols = pl.ds(pl.multiple_of(mine * width, LANE), width)

    def core_copies(index, slot):
        made = []
        for d in range(1, grp):
            made.append(
                pltpu.make_async_remote_copy(
                    src_ref=out_ref.at[index, :, cols],
                    dst_ref=out_ref.at[index, :, cols],
                    send_sem=csend.at[slot * (grp - 1) + d - 1],
                    recv_sem=crecv.at[slot * (grp - 1) + d - 1],
                    device_id=((mine + d) % grp, me),
                    device_id_type=MESH,
                )
            )
        return made

    started, cores = [], []
    held = [(me, None)]
    slot = 0
    for w in worths:
        side = (me // w) % 2
        step = (1 - 2 * side) * w
        coming = []
        for index, arrival in held:
            if arrival is not None and not arrival[2][0]:
                _land(arrival, index, core_copies, cores)
            pair = []
            for ref, sends, recvs in (
                (out_ref.at[index, :, cols], send_sem, recv_sem),
                (pos_ref.at[index], psend, precv),
            ):
                pair.append(
                    pltpu.make_async_remote_copy(
                        src_ref=ref,
                        dst_ref=ref,
                        send_sem=sends.at[slot],
                        recv_sem=recvs.at[slot],
                        device_id=(mine, me + step),
                        device_id_type=MESH,
                    )
                )
            for c in pair:
                c.start()
            started += pair
            coming.append((index + step, (pair, slot, [False])))
            slot += 1
        held = held + coming
    for index, arrival in held:
        if arrival is not None and not arrival[2][0]:
            _land(arrival, index, core_copies, cores)
    for c in started:
        c.wait_send()
    for c in cores:
        c.wait()


def _land(arrival, index, core_copies, cores):
    pair, slot, done = arrival
    for c in pair:
        c.wait_recv()
    more = core_copies(index, slot)
    for c in more:
        c.start()
    cores.extend(more)
    done[0] = True


def _merge_stats(a, b):
    lane = lax.broadcasted_iota(jnp.int32, a.shape, 1)
    top = jnp.maximum(a, b)
    wa = pltpu.roll(a, LANE - QUERY_HEADS, 1) * jnp.exp2(a - top)
    wb = pltpu.roll(b, LANE - QUERY_HEADS, 1) * jnp.exp2(b - top)
    wa = jnp.where(lane < QUERY_HEADS, wa, 0.0)
    wb = jnp.where(lane < QUERY_HEADS, wb, 0.0)
    den = wa + wb
    inverse = 1.0 / jnp.maximum(den, TINY)
    merged = jnp.where(lane < QUERY_HEADS, top, pltpu.roll(den, QUERY_HEADS, 1))
    return wa * inverse, wb * inverse, merged


def _reduce_kernel(
    blk, grp, acc_in, st_in, out_ref, acc, st, stage, stage_st, land, land_st, final, sends, recvs, ssends, srecvs, fsend, frecv
):
    me, mine = lax.axis_index("blk"), lax.axis_index("grp")
    bits, gbits = blk.bit_length() - 1, grp.bit_length() - 1
    worths = _orders(mine, bits)
    rows, total = acc_in.shape[1], acc_in.shape[2]
    _greet(me, mine, grp, worths)
    width = total
    origin = 0
    number = 0
    wire = stage.dtype
    source, source_st = acc_in, st_in
    at = 0
    at_st = 0
    waits = []

    def send(size_cols, first, count, device):
        nonlocal number
        made = (
            pltpu.make_async_remote_copy(
                src_ref=stage.at[pl.ds(first, count)],
                dst_ref=land.at[pl.ds(first, count)],
                send_sem=sends.at[number],
                recv_sem=recvs.at[number],
                device_id=device,
                device_id_type=MESH,
            ),
            pltpu.make_async_remote_copy(
                src_ref=stage_st.at[pl.ds(at_st, count // (size_cols // unit))],
                dst_ref=land_st.at[pl.ds(at_st, count // (size_cols // unit))],
                send_sem=ssends.at[number],
                recv_sem=srecvs.at[number],
                device_id=device,
                device_id_type=MESH,
            ),
        )
        number += 1
        for c in made:
            c.start()
        waits.extend(made)
        return made

    unit = total // grp
    for b in range(gbits):
        half = width // 2
        side = (mine // 2**b) % 2
        partner = mine + (1 - 2 * side) * 2**b
        keep = pl.multiple_of(origin + side * half, LANE)
        give = pl.multiple_of(origin + (1 - side) * half, LANE)
        parts = half // unit
        base, base_st = at, at_st

        def pack(i, c):
            for p in range(parts):
                stage[base + i * parts + p] = source[i, :, pl.ds(pl.multiple_of(give + p * unit, LANE), unit)].astype(wire)
            stage_st[base_st + i] = source_st[i]
            return c

        lax.fori_loop(0, blk, pack, 0)
        made = send(half, at, blk * parts, (partner, me))
        for c in made:
            c.wait_recv()
        heads = half // HEAD_SIZE
        first_head = keep // HEAD_SIZE

        def merge(i, c):
            ca, cb, both = _merge_stats(source_st[i], land_st[base_st + i])
            shift = (LANE - first_head) % LANE
            ca, cb = pltpu.roll(ca, shift, 1), pltpu.roll(cb, shift, 1)
            for h in range(heads):
                p, o = divmod(h * HEAD_SIZE, unit)
                acc[i, :, pl.ds(pl.multiple_of(keep + h * HEAD_SIZE, LANE), HEAD_SIZE)] = (
                    ca[:, h : h + 1] * source[i, :, pl.ds(pl.multiple_of(keep + h * HEAD_SIZE, LANE), HEAD_SIZE)]
                    + cb[:, h : h + 1] * land[base + i * parts + p, :, o : o + HEAD_SIZE].astype(jnp.float32)
                )
            st[i] = both
            return c

        lax.fori_loop(0, blk, merge, 0)
        source, source_st = acc, st
        origin = keep
        width = half
        at += blk * parts
        at_st += blk
    cols = pl.ds(pl.multiple_of(origin, LANE), unit)
    first_head = origin // HEAD_SIZE
    shift = (LANE - first_head) % LANE
    heads = unit // HEAD_SIZE
    count = blk
    for s, w in enumerate(worths):
        side = (me // w) % 2
        partner = me + (1 - 2 * side) * w
        place = (w if s == 0 else 1)
        half = count // 2
        base, base_st = at, at_st

        def pick(i, which):
            return (i // place) * (2 * place) + which * place + i % place

        def pack(i, c):
            j = pick(i, 1 - side)
            stage[base + i] = acc[j, :, cols].astype(wire)
            stage_st[base_st + i] = st[j]
            return c

        lax.fori_loop(0, half, pack, 0)
        made = send(unit, at, half, (mine, partner))
        for c in made:
            c.wait_recv()

        def merge(i, c):
            j = pick(i, side)
            ca, cb, both = _merge_stats(st[j], land_st[base_st + i])
            ca, cb = pltpu.roll(ca, shift, 1), pltpu.roll(cb, shift, 1)
            for h in range(heads):
                o = pl.ds(pl.multiple_of(origin + h * HEAD_SIZE, LANE), HEAD_SIZE)
                acc[i, :, o] = ca[:, h : h + 1] * acc[j, :, o] + cb[:, h : h + 1] * land[
                    base + i, :, h * HEAD_SIZE : (h + 1) * HEAD_SIZE
                ].astype(jnp.float32)
            st[i] = both
            return c

        lax.fori_loop(0, half, merge, 0)
        count = half
        at += half
        at_st += half
    final[mine] = acc[0, :, cols].astype(jnp.bfloat16)
    last = []
    for d in range(1, grp):
        c = pltpu.make_async_remote_copy(
            src_ref=final.at[mine],
            dst_ref=final.at[mine],
            send_sem=fsend.at[d - 1],
            recv_sem=frecv.at[d - 1],
            device_id=((mine + d) % grp, me),
            device_id_type=MESH,
        )
        c.start()
        last.append(c)
    for c in waits:
        c.wait_send()
    for c in last:
        c.wait()
    for g in range(grp):
        p = sum(((g >> b) & 1) << (gbits - 1 - b) for b in range(gbits))
        out_ref[:, p * unit : (p + 1) * unit] = final[g]


def on_device(
    queries, turn_pos, cached_key_rows, cached_value_rows, turn_keys, turn_values, cache_pos
):
    blk = lax.axis_size("blk")
    grp = lax.axis_size("grp")
    slots = cached_key_rows.shape[0]
    width = cached_key_rows.shape[1]
    fresh = turn_keys.shape[0]
    base = slots * grp * blk // 2
    size = -(-(slots + fresh) // LANE) * LANE + 2 * BLOCK
    rows_in = queries.shape[0]
    vmem = pl.BlockSpec(memory_space=pltpu.VMEM)
    moves = blk - 1
    limit_rows = jnp.broadcast_to((turn_pos - base + 1).astype(jnp.float32)[:, None], (rows_in, LANE))
    every_query, limits = pl.pallas_call(
        functools.partial(_gather_kernel, blk, grp),
        out_shape=(
            jax.ShapeDtypeStruct((blk, rows_in, queries.shape[1]), jnp.bfloat16),
            jax.ShapeDtypeStruct((blk, rows_in, LANE), jnp.float32),
        ),
        in_specs=[vmem, vmem],
        out_specs=(vmem, vmem),
        scratch_shapes=[pltpu.SemaphoreType.DMA]
        + [pltpu.SemaphoreType.DMA((moves,))] * 4
        + [pltpu.SemaphoreType.DMA((moves * (grp - 1),))] * 2,
        compiler_params=pltpu.CompilerParams(
            collective_id=0, has_side_effects=True, vmem_limit_bytes=24 * 2**20
        ),
        name="gather",
    )(queries, limit_rows)
    every_query = every_query.reshape(blk * rows_in, queries.shape[1])
    limits = limits.reshape(blk * rows_in, LANE)
    tokens = every_query.shape[0]
    pad = ((0, LANE - fresh), (0, 0))
    smem = pl.BlockSpec(memory_space=pltpu.SMEM)
    kc, vc, code, count = pl.pallas_call(
        functools.partial(_compact_kernel, base, slots, fresh),
        out_shape=(
            jax.ShapeDtypeStruct((size, width), jnp.bfloat16),
            jax.ShapeDtypeStruct((size, width), jnp.bfloat16),
            jax.ShapeDtypeStruct((16, size), jnp.float32),
            jax.ShapeDtypeStruct((2,), jnp.int32),
        ),
        in_specs=[vmem] * 5,
        out_specs=(vmem, vmem, vmem, smem),
        compiler_params=pltpu.CompilerParams(vmem_limit_bytes=40 * 2**20),
        name="compact",
    )(
        cache_pos.reshape(slots // LANE, LANE),
        cached_key_rows,
        cached_value_rows,
        jnp.pad(turn_keys, pad),
        jnp.pad(turn_values, pad),
    )
    rank = lax.axis_index(("grp", "blk"))
    first = (rank * fresh).astype(jnp.int32).reshape(1)
    rows = GROUP * tokens
    accum, stats = pl.pallas_call(
        functools.partial(_attend_kernel, fresh),
        out_shape=(
            jax.ShapeDtypeStruct((tokens, QUERY_HEADS * HEAD_SIZE), jnp.float32),
            jax.ShapeDtypeStruct((tokens, LANE), jnp.float32),
        ),
        in_specs=[smem] * 2 + [vmem] * 5,
        out_specs=(vmem, vmem),
        scratch_shapes=[
            pltpu.VMEM((size // LANE, rows, LANE), jnp.float32),
            pltpu.VMEM((rows, LANE), jnp.float32),
            pltpu.VMEM((rows, LANE), jnp.float32),
        ],
        compiler_params=pltpu.CompilerParams(vmem_limit_bytes=56 * 2**20),
        name="attend",
    )(count, first, every_query, kc, vc, code, limits)
    unit = QUERY_HEADS * HEAD_SIZE // grp
    blocks = blk * (grp - 1) + blk - 1
    stat_blocks = blk * (grp.bit_length() - 1) + blk - 1
    steps = blk.bit_length() + grp.bit_length() - 2
    wire = jnp.float32
    return pl.pallas_call(
        functools.partial(_reduce_kernel, blk, grp),
        out_shape=jax.ShapeDtypeStruct((rows_in, QUERY_HEADS * HEAD_SIZE), jnp.bfloat16),
        in_specs=[vmem] * 2,
        out_specs=vmem,
        scratch_shapes=[
            pltpu.VMEM((blk, rows_in, QUERY_HEADS * HEAD_SIZE), jnp.float32),
            pltpu.VMEM((blk, rows_in, LANE), jnp.float32),
            pltpu.VMEM((blocks, rows_in, unit), wire),
            pltpu.VMEM((stat_blocks, rows_in, LANE), jnp.float32),
            pltpu.VMEM((blocks, rows_in, unit), wire),
            pltpu.VMEM((stat_blocks, rows_in, LANE), jnp.float32),
            pltpu.VMEM((grp, rows_in, unit), jnp.bfloat16),
        ]
        + [pltpu.SemaphoreType.DMA((steps,))] * 4
        + [pltpu.SemaphoreType.DMA((grp - 1,))] * 2,
        compiler_params=pltpu.CompilerParams(
            collective_id=1, has_side_effects=True, vmem_limit_bytes=48 * 2**20
        ),
        name="reduce",
    )(
        accum.reshape(blk, rows_in, QUERY_HEADS * HEAD_SIZE),
        stats.reshape(blk, rows_in, LANE),
    )


def solution(mesh):
    placed = (
        P("blk", None),
        P("blk"),
        P(("grp", "blk"), None),
        P(("grp", "blk"), None),
        P(("grp", "blk"), None),
        P(("grp", "blk"), None),
        P(("grp", "blk")),
    )
    return jax.shard_map(
        on_device, mesh=mesh, in_specs=placed, out_specs=P("blk", None), check_vma=False
    )
```
